256 devices in a mesh: dp: 16 (over z_hi, y, core), tensor: 16 (over z_lo, x).
Axes of the slice: x: 4, y: 4, z: 8 (z_hi: 2, z_lo: 4; z = z_hi * 4 + z_lo), core: 2. Of those that a mesh axis runs over, the one named last changes fastest.
Arguments:
- hidden: bfloat16 [2048, 26624], P('dp', 'tensor'), parts along dimension 0, may hold values from -6 to 6
- residual: bfloat16 [2048, 8320], P(('dp', 'tensor')), parts along dimension 0, may hold values from -6 to 6
- sign_bits: int32 [26624], P('tensor'), may hold values from 0 to 1
- packed: float32 [26624, 1664], P('tensor'), may hold values from 0 to 1048575, as said below
- scales: float32 [8320], replicated, may hold values from 0.0006 to 0.004
Outputs:
- layer_out: bfloat16 [2048, 8320], P(('dp', 'tensor')), parts along dimension 0
The draws below stay inside these ranges and needn't reach their ends.
There are 16 independent parts, one for each index of `dp`. The reference program is written for one: setup_inputs(seed, part) draws one part's arguments, and reference() takes and returns one part's arrays. A program takes and returns all parts, laid end to end along the dimension named above; an argument that names none is the same for every part. Nothing has to cross between parts.
Inputs may be any that keep to these rules, and one draw needn't show every extreme that they name: `sign_bits`: 0 flips the sign of a hidden unit before the rotation. `packed`: each word is a whole number; its base-16 digit k holds the code plus 8 of output feature 5j+k for hidden unit f, k = 0 to 4.
All inputs are finite; a program needn't handle non-finite values.
Results may differ from the reference program's by a relative error of at most 0.025.
Values may be sent and summed in bfloat16 or wider, within the bound.
A program may use at most 192 MiB of HBM per device.

```python
import math
import jax
import jax.numpy as jnp
from jax import lax

WALSH = 2048
ODD = 13
D_WIN = 8320
TOK = 128
FF = 26624
N_TENSOR = 16


def draw_packed(key, part):
    key = jax.random.fold_in(key, 11)
    words = jax.random.randint(key, (FF, D_WIN // 5), 0, 1048576, dtype=jnp.int32)
    return words.astype(jnp.float32)


def set_ends(values, own_key, low, largest):
    spot = [jax.random.randint(jax.random.fold_in(own_key, axis), (), 0, length) for axis, length in enumerate(values.shape)]
    widest = values.shape.index(max(values.shape))
    neighbour = spot[:widest] + [(spot[widest] + 1) % values.shape[widest]] + spot[widest + 1:]
    return values.at[tuple(spot)].set(low).at[tuple(neighbour)].set(largest)


def steps_of(stream_key, shape, pieces, low, high):
    level = 1.0
    for position, blocks in pieces:
        heights = jax.random.uniform(jax.random.fold_in(jax.random.fold_in(stream_key, 6), position), (blocks,), jnp.float32, low / len(pieces), high / len(pieces))
        level = level * jnp.repeat(jnp.exp(heights), shape[position] // blocks).reshape((-1,) + (1,) * (len(shape) - 1 - position))
    return level


def normal_values(own_key, shape, width, reach, split=(), kind=jnp.bfloat16):
    result = width * jax.random.normal(own_key, shape, jnp.float32)
    if split:
        result = result * steps_of(own_key, shape, split, -0.22, 0.18)
    return jnp.clip(result, -reach, reach).astype(kind)


def setup_inputs(seed: int = 0, part: int = 0) -> dict:
    splits = jax.random.split(jax.random.key(seed), 6)
    own_keys = jax.random.split(jax.random.fold_in(splits[5], part), 6)
    hidden = normal_values(own_keys[0], (TOK, FF), 1.0, 6.0, ((1, 16),))
    residual = normal_values(own_keys[1], (TOK, D_WIN), 1.0, 6.0, ((0, 16),))
    sign_bits = set_ends(jax.random.randint(splits[2], (FF,), 0, 2), jax.random.fold_in(splits[2], 1), 0, 1).astype(jnp.int32)
    packed = draw_packed(jax.random.fold_in(splits[5], 71), part)
    scales = jnp.clip(jnp.exp(jax.random.uniform(splits[4], (D_WIN,), jnp.float32, math.log(0.0006), math.log(0.004))), 0.0006, 0.004)
    return {"hidden": hidden, "residual": residual, "sign_bits": sign_bits, "packed": packed, "scales": scales}


def dct_table():
    frequency = jnp.arange(ODD, dtype=jnp.float32)[:, None]
    sample = jnp.arange(ODD, dtype=jnp.float32)[None, :]
    weights = jnp.where(frequency == 0, math.sqrt(0.5), 1.0) * math.sqrt(2.0 / ODD)
    return weights * jnp.cos(math.pi * (2.0 * sample + 1.0) * frequency / (2.0 * ODD))

def rotate(flipped):
    tokens = flipped.shape[0]
    values = flipped.astype(jnp.float32).reshape(tokens, WALSH, ODD)
    for section_no in range(WALSH.bit_length() - 1):
        span_len = 2 ** section_no
        viewed = values.reshape(tokens, WALSH // (2 * span_len), 2, span_len, ODD)
        front_half = viewed[:, :, 0]
        back_half = viewed[:, :, 1]
        values = jnp.stack([front_half + back_half, front_half - back_half], axis=2).reshape(tokens, WALSH, ODD)
    turned = jnp.einsum('tab,kb->tak', values, dct_table(), precision=lax.Precision.HIGHEST)
    return (turned / math.sqrt(WALSH)).reshape(tokens, WALSH * ODD)

def unpack(packed_rows):
    digits = [jnp.mod(jnp.floor_divide(packed_rows, 16.0 ** place), 16.0) - 8.0 for place in range(5)]
    stacked = jnp.stack(digits, axis=2)
    return stacked.reshape(packed_rows.shape[0], packed_rows.shape[1] * 5).astype(jnp.bfloat16)

def reference(hidden, residual, sign_bits, packed, scales):
    sign_flips = (2 * sign_bits - 1).astype(jnp.bfloat16)
    flipped = hidden * sign_flips[None, :]
    rotated = rotate(flipped).astype(jnp.bfloat16)
    block_rows = FF // N_TENSOR

    def one_block(running, block_index):
        rows = lax.dynamic_slice_in_dim(rotated, block_index * block_rows, block_rows, 1)
        packed_rows = lax.dynamic_slice_in_dim(packed, block_index * block_rows, block_rows, 0)
        weight_codes = unpack(packed_rows)
        block_term = jnp.dot(rows, weight_codes, preferred_element_type=jnp.float32) * scales[None, :]
        rounded = lax.optimization_barrier(block_term.astype(jnp.bfloat16))
        return (running + rounded.astype(jnp.float32), None)
    start = jnp.zeros((hidden.shape[0], D_WIN), jnp.float32)
    summed, _ = lax.scan(one_block, start, jnp.arange(N_TENSOR, dtype=jnp.int32))
    return (residual.astype(jnp.float32) + summed).astype(jnp.bfloat16)
```

```python
import math

import jax
import jax.numpy as jnp
import numpy as np
from jax import lax
from jax.experimental import pallas as pl
from jax.experimental.pallas import tpu as pltpu
from jax.sharding import PartitionSpec as P

WALSH = 2048
ODD = 13
GROUPS = 16
NX = 4
NZ = 4
TOK = 128
ROW = 1664
DIGITS = 5
LANE = 128
WIDE = 2 * LANE
PAIRS = 7
TILES = 13
BLOCK = DIGITS * LANE
SLOTS = 4
MESH = pl.DeviceIdType.MESH
F32 = jnp.float32
BF16 = jnp.bfloat16


def turn_table():
    local = ROW // ODD
    ids = np.arange(local)
    both = ids[:, None] & ids[None, :]
    parity = np.zeros_like(both)
    for bit in range(local.bit_length() - 1):
        parity ^= (both >> bit) & 1
    walsh = 1.0 - 2.0 * parity
    k = np.arange(ODD)[:, None]
    b = np.arange(ODD)[None, :]
    cosine = np.where(k == 0, math.sqrt(0.5), 1.0) * math.sqrt(2.0 / ODD)
    cosine = cosine * np.cos(math.pi * (2.0 * b + 1.0) * k / (2.0 * ODD))
    return (np.kron(walsh, cosine.T) / math.sqrt(WALSH)).astype(jnp.bfloat16)


def peers(me):
    z, x = me // NX, me % NX
    out = []
    for dz in (2, 1, 3, 0):
        for dx in (2, 1, 3, 0):
            if dz or dx:
                out.append((dz * NX + dx, (z + dz) % NZ * NX + (x + dx) % NX))
    return out


def kernel(
    hid, res, sgn, packed, scl, turn, out,
    hid_v, res_v, sgn_v, scl_v, turn_v, words, codes, perm,
    rx, mixed, tx, rr, lhs, part, in1, out2, in2, summed, in3, fin,
    load_sem, word_sem, s1, r1, s2, r2, sx1, rx1, sx2, rx2, sz, rz,
):
    me = lax.axis_index("tensor")
    z, x = me // NX, me % NX
    loads = []
    for n, (src, dst) in enumerate(
        ((hid, hid_v), (sgn, sgn_v), (turn, turn_v), (res, res_v), (scl, scl_v))
    ):
        loads.append(pltpu.make_async_copy(src, dst, load_sem.at[n]))

    def word_copy(r, slot):
        return pltpu.make_async_copy(
            packed.at[pl.ds(pl.multiple_of(r * LANE, LANE), LANE)], words.at[slot], word_sem.at[slot]
        )

    loads[0].start()
    loads[1].start()
    barrier = pltpu.get_barrier_semaphore()
    for _, peer in peers(me):
        pl.semaphore_signal(barrier, inc=1, device_id={"tensor": peer}, device_id_type=MESH)
    for r in range(SLOTS):
        word_copy(r, r).start()
    for n in (2, 3, 4):
        loads[n].start()

    loads[0].wait()
    loads[1].wait()
    flips = (2 * sgn_v[...] - 1).astype(F32)

    @pl.loop(0, GROUPS)
    def _(g):
        hid_v[g] = (hid_v[g].astype(F32) * flips).astype(BF16)

    pl.semaphore_wait(barrier, GROUPS - 1)

    def send(src, dst, sem_s, sem_r):
        copies = []
        for off, peer in peers(me):
            copy = pltpu.make_async_remote_copy(
                src_ref=src.at[peer], dst_ref=dst.at[me], send_sem=sem_s.at[off], recv_sem=sem_r.at[off],
                device_id={"tensor": peer}, device_id_type=MESH,
            )
            copy.start()
            copies.append(copy)
        return copies

    def unpack(r):
        slot = r % SLOTS
        word_copy(r, slot).wait()
        rows = pl.ds(pl.multiple_of(r * LANE, LANE), LANE)
        for p in range(PAIRS):
            wide = WIDE if p < PAIRS - 1 else LANE
            word = words[slot, :, p * WIDE : p * WIDE + wide].astype(jnp.int32) ^ 0x88888
            for k in range(DIGITS):
                digit = (word << (28 - 4 * k)) >> 28
                codes[p * DIGITS + k, rows, :wide] = digit.astype(F32).astype(BF16)

        @pl.when(r + SLOTS < TILES)
        def _():
            word_copy(r + SLOTS, slot).start()

    sent1 = send(hid_v, rx, s1, r1)
    rx[me] = hid_v[me]
    first_rows = 6

    @pl.loop(0, first_rows)
    def _(r):
        unpack(r)

    rows = lax.broadcasted_iota(jnp.int32, (BLOCK, BLOCK), 0)
    cols = lax.broadcasted_iota(jnp.int32, (BLOCK, BLOCK), 1)
    perm[...] = jnp.where((rows & (LANE - 1)) * DIGITS + (rows >> 7) == cols, 1.0, 0.0).astype(BF16)
    fin[...] = jnp.zeros_like(fin)

    for copy in sent1:
        copy.wait_recv()

    @pl.loop(0, TILES)
    def _(c):
        lanes = pl.ds(pl.multiple_of(c * LANE, LANE), LANE)
        blocks = [rx[g, :, lanes].astype(F32) for g in range(GROUPS)]
        span = 1
        while span < GROUPS:
            for g in range(GROUPS):
                if not g & span:
                    a, b = blocks[g], blocks[g + span]
                    blocks[g], blocks[g + span] = a + b, a - b
            span *= 2
        mixed[:, lanes] = jnp.concatenate(blocks, axis=0).astype(BF16)

    loads[2].wait()

    def turned(start, wide):
        lanes = pl.ds(start, wide)
        y = jnp.dot(mixed[...], turn_v[:, lanes], preferred_element_type=F32)
        tx[:, :, lanes] = y.reshape(GROUPS, TOK // GROUPS, wide).astype(BF16)

    @pl.loop(0, PAIRS - 1)
    def _(c):
        turned(pl.multiple_of(c * WIDE, WIDE), WIDE)

    turned((PAIRS - 1) * WIDE, LANE)
    sent2 = send(tx, rr, s2, r2)
    rr[me] = tx[me]

    @pl.loop(first_rows, TILES)
    def _(r):
        unpack(r)

    loads[3].wait()
    loads[4].wait()
    for copy in sent2:
        copy.wait_recv()

    @pl.loop(0, TILES)
    def _(c):
        lanes = pl.ds(pl.multiple_of(c * LANE, LANE), LANE)
        lhs[:, lanes] = rr[:, :, lanes].astype(F32).reshape(TOK, LANE).astype(BF16)

    across = (x + 1 - 2 * (x % 2), 3 - x)
    half = ((x + 1) // 2 % 2, x // 2)
    mine = (x // 2, x % 2)
    place = ((0, 2, 3, 1), (0, 1, 2, 3))

    def first(p, t):
        return pltpu.make_async_remote_copy(
            src_ref=part.at[p, t, pl.ds(2 * (1 - half[t]), 2)], dst_ref=in1.at[p, t],
            send_sem=sx1.at[p, t], recv_sem=rx1.at[p, t],
            device_id={"tensor": z * NX + across[t]}, device_id_type=MESH,
        )

    def second(p, t):
        return pltpu.make_async_remote_copy(
            src_ref=out2.at[p, t], dst_ref=in2.at[p, t], send_sem=sx2.at[p, t], recv_sem=rx2.at[p, t],
            device_id={"tensor": z * NX + across[1 - t]}, device_id_type=MESH,
        )

    def third(p, dz, tiles):
        there = (z + dz) % NZ
        return pltpu.make_async_remote_copy(
            src_ref=summed.at[p, there, pl.ds(0, tiles)], dst_ref=in3.at[p, dz - 1, pl.ds(0, tiles)],
            send_sem=sz.at[p, dz - 1], recv_sem=rz.at[p, dz - 1],
            device_id={"tensor": there * NX + x}, device_id_type=MESH,
        )

    def multiply(p, tiles):
        for k in range(DIGITS):
            y = jnp.dot(lhs[...], codes[p * DIGITS + k, :, : tiles * LANE], preferred_element_type=F32)
            y = y.reshape(NZ, NX, TOK // GROUPS, tiles * LANE)
            for t in range(tiles):
                for xx in range(NX):
                    part[p, t, place[t][xx], :, :, k * LANE : (k + 1) * LANE] = y[
                        :, xx, :, t * LANE : (t + 1) * LANE
                    ].astype(BF16)
        for t in range(tiles):
            first(p, t).start()

    def halve(p, tiles):
        for t in range(tiles):
            first(p, t).wait_recv()
            other = 1 - mine[t]
            out2[p, t] = (
                part[p, t, 2 * half[t] + other].astype(F32) + in1[p, t, other].astype(F32)
            ).astype(BF16)
            second(p, t).start()

    def spread(p, tiles):
        for t in range(tiles):
            second(p, t).wait_recv()
            total = part[p, t, 2 * half[t] + mine[t]].astype(F32) + in1[p, t, mine[t]].astype(F32)
            summed[p, :, t] = (total + in2[p, t].astype(F32)).astype(BF16)
        for dz in (2, 1, 3):
            third(p, dz, tiles).start()

    def gather(p, tiles):
        for dz in (2, 1, 3):
            third(p, dz, tiles).wait_recv()
        total = summed[p, z, :tiles].astype(F32)
        for n in range(NZ - 1):
            total = total + in3[p, n, :tiles].astype(F32)
        total = total.reshape(tiles * 8, BLOCK)
        if tiles == 1:
            total = jnp.concatenate([total, jnp.zeros_like(total)], axis=0)
        high = total.astype(BF16)
        rows = pl.ds(pl.multiple_of(p * 16, 16), 16)
        fin[0, rows, :] = high
        fin[1, rows, :] = (total - high.astype(F32)).astype(BF16)

    stages = (multiply, halve, spread, gather)
    lags = (0, 1, 2, 3)
    last = PAIRS - 1
    for p in range(lags[-1]):
        for stage, lag in zip(stages, lags):
            if p >= lag:
                stage(p - lag, 2)

    @pl.loop(lags[-1], last)
    def _(p):
        for stage, lag in zip(stages, lags):
            stage(p - lag, 2)

    for p in range(last, last + lags[-1] + 1):
        for stage, lag in zip(stages, lags):
            if p - lag <= last:
                stage(p - lag, 2 if p - lag < last else 1)

    y = jnp.dot(fin[...].reshape(2 * PAIRS * 16, BLOCK), perm[...], preferred_element_type=F32)
    y = y[: PAIRS * 16] + y[PAIRS * 16 :]
    for t in range(TILES):
        lanes = pl.ds(t * BLOCK, BLOCK)
        out[:, lanes] = (
            res_v[:, lanes].astype(F32) + y[8 * t : 8 * t + 8] * scl_v[:, lanes]
        ).astype(BF16)

    for copy in sent1 + sent2:
        copy.wait_send()

    @pl.loop(0, last)
    def _(p):
        for t in range(2):
            first(p, t).wait_send()
            second(p, t).wait_send()
        for dz in (1, 2, 3):
            third(p, dz, 2).wait_send()

    first(last, 0).wait_send()
    second(last, 0).wait_send()
    for dz in (1, 2, 3):
        third(last, dz, 1).wait_send()


def shards(hidden, residual, sign_bits, packed, scales):
    width = BLOCK * TILES
    dma = pltpu.SemaphoreType.DMA
    vmem = pltpu.VMEM
    tok = TOK // GROUPS
    return pl.pallas_call(
        kernel,
        out_shape=jax.ShapeDtypeStruct((tok, width), BF16),
        in_specs=[pl.BlockSpec(memory_space=pl.ANY)] * 6,
        out_specs=pl.BlockSpec(memory_space=pltpu.VMEM),
        scratch_shapes=[
            vmem((GROUPS, tok, ROW), BF16),
            vmem((tok, width), BF16),
            vmem((1, ROW), jnp.int32),
            vmem((1, width), F32),
            vmem((ROW, ROW), BF16),
            vmem((SLOTS, LANE, ROW), F32),
            vmem((PAIRS * DIGITS, ROW, WIDE), BF16),
            vmem((BLOCK, BLOCK), BF16),
            vmem((GROUPS, tok, ROW), BF16),
            vmem((TOK, ROW), BF16),
            vmem((GROUPS, tok, ROW), BF16),
            vmem((GROUPS, tok, ROW), BF16),
            vmem((TOK, ROW), BF16),
            vmem((PAIRS, 2, NX, NZ, tok, BLOCK), BF16),
            vmem((PAIRS, 2, 2, NZ, tok, BLOCK), BF16),
            vmem((PAIRS, 2, NZ, tok, BLOCK), BF16),
            vmem((PAIRS, 2, NZ, tok, BLOCK), BF16),
            vmem((PAIRS, NZ, 2, tok, BLOCK), BF16),
            vmem((PAIRS, NZ - 1, 2, tok, BLOCK), BF16),
            vmem((2, PAIRS * 16, BLOCK), BF16),
            dma((5,)),
            dma((SLOTS,)),
            dma((GROUPS,)),
            dma((GROUPS,)),
            dma((GROUPS,)),
            dma((GROUPS,)),
            dma((PAIRS, 2)),
            dma((PAIRS, 2)),
            dma((PAIRS, 2)),
            dma((PAIRS, 2)),
            dma((PAIRS, NZ - 1)),
            dma((PAIRS, NZ - 1)),
        ],
        compiler_params=pltpu.CompilerParams(
            collective_id=0, has_side_effects=True, vmem_limit_bytes=60 * 1024 * 1024
        ),
        cost_estimate=pl.CostEstimate(flops=4_300_000_000, bytes_accessed=17_000_000, transcendentals=0),
    )(
        hidden.reshape(GROUPS, tok, ROW),
        residual,
        sign_bits.reshape(1, ROW),
        packed,
        scales.reshape(1, width),
        jnp.asarray(turn_table()),
    )


def solution(mesh):
    return jax.shard_map(
        shards,
        mesh=mesh,
        in_specs=(
            P("dp", "tensor"),
            P(("dp", "tensor"), None),
            P("tensor"),
            P("tensor", None),
            P(),
        ),
        out_specs=P(("dp", "tensor"), None),
        check_vma=False,
    )
```

```python
import math

import jax
import jax.numpy as jnp
import numpy as np
from jax import lax
from jax.experimental import pallas as pl
from jax.experimental.pallas import tpu as pltpu
from jax.sharding import PartitionSpec as P

WALSH = 2048
ODD = 13
GROUPS = 16
NX = 4
NZ = 4
TOK = 128
ROW = 1664
DIGITS = 5
LANE = 128
WIDE = 2 * LANE
PAIRS = 7
TILES = 13
BLOCK = DIGITS * LANE
SLOTS = 4
MESH = pl.DeviceIdType.MESH
F32 = jnp.float32
BF16 = jnp.bfloat16


def turn_table():
    local = ROW // ODD
    ids = np.arange(local)
    both = ids[:, None] & ids[None, :]
    parity = np.zeros_like(both)
    for bit in range(local.bit_length() - 1):
        parity ^= (both >> bit) & 1
    walsh = 1.0 - 2.0 * parity
    k = np.arange(ODD)[:, None]
    b = np.arange(ODD)[None, :]
    cosine = np.where(k == 0, math.sqrt(0.5), 1.0) * math.sqrt(2.0 / ODD)
    cosine = cosine * np.cos(math.pi * (2.0 * b + 1.0) * k / (2.0 * ODD))
    return (np.kron(walsh, cosine.T) / math.sqrt(WALSH)).astype(jnp.bfloat16)


def peers(me):
    z, x = me // NX, me % NX
    out = []
    for dz in (2, 1, 3, 0):
        for dx in (2, 1, 3, 0):
            if dz or dx:
                out.append((dz * NX + dx, (z + dz) % NZ * NX + (x + dx) % NX))
    return out


def kernel(
    hid, res, sgn, packed, scl, turn, out,
    hid_v, res_v, sgn_v, scl_v, turn_v, words, codes, perm,
    rx, mixed, tx, rr, lhs, part, in1, out2, in2, summed, in3, fin,
    load_sem, word_sem, s1, r1, s2, r2, sx1, rx1, sx2, rx2, sz, rz,
):
    me = lax.axis_index("tensor")
    z, x = me // NX, me % NX
    loads = []
    for n, (src, dst) in enumerate(
        ((hid, hid_v), (sgn, sgn_v), (turn, turn_v), (res, res_v), (scl, scl_v))
    ):
        loads.append(pltpu.make_async_copy(src, dst, load_sem.at[n]))

    def word_copy(r, slot):
        return pltpu.make_async_copy(
            packed.at[pl.ds(pl.multiple_of(r * LANE, LANE), LANE)], words.at[slot], word_sem.at[slot]
        )

    loads[0].start()
    loads[1].start()
    barrier = pltpu.get_barrier_semaphore()
    for _, peer in peers(me):
        pl.semaphore_signal(barrier, inc=1, device_id={"tensor": peer}, device_id_type=MESH)
    for r in range(SLOTS):
        word_copy(r, r).start()
    for n in (2, 3, 4):
        loads[n].start()

    loads[0].wait()
    loads[1].wait()

    @pl.loop(0, TILES)
    def _(c):
        lanes = pl.ds(pl.multiple_of(c * LANE, LANE), LANE)
        flips = (2 * sgn_v[lanes] - 1).astype(F32).reshape(1, LANE)
        hid_v[:, :, lanes] = (hid_v[:, :, lanes].astype(F32) * flips).astype(BF16)

    pl.semaphore_wait(barrier, GROUPS - 1)

    def send(src, dst, sem_s, sem_r):
        copies = []
        for off, peer in peers(me):
            copy = pltpu.make_async_remote_copy(
                src_ref=src.at[peer], dst_ref=dst.at[me], send_sem=sem_s.at[off], recv_sem=sem_r.at[off],
                device_id={"tensor": peer}, device_id_type=MESH,
            )
            copy.start()
            copies.append(copy)
        return copies

    def unpack(r):
        slot = r % SLOTS
        word_copy(r, slot).wait()
        rows = pl.ds(pl.multiple_of(r * LANE, LANE), LANE)
        for p in range(PAIRS):
            wide = WIDE if p < PAIRS - 1 else LANE
            word = words[slot, :, p * WIDE : p * WIDE + wide].astype(jnp.int32) ^ 0x88888
            for k in range(DIGITS):
                digit = (word << (28 - 4 * k)) >> 28
                codes[p * DIGITS + k, rows, :wide] = digit.astype(F32).astype(BF16)

        @pl.when(r + SLOTS < TILES)
        def _():
            word_copy(r + SLOTS, slot).start()

    sent1 = send(hid_v, rx, s1, r1)
    rx[me] = hid_v[me]
    first_rows = 6

    @pl.loop(0, first_rows)
    def _(r):
        unpack(r)

    rows = lax.broadcasted_iota(jnp.int32, (BLOCK, BLOCK), 0)
    cols = lax.broadcasted_iota(jnp.int32, (BLOCK, BLOCK), 1)
    perm[...] = jnp.where((rows & (LANE - 1)) * DIGITS + (rows >> 7) == cols, 1.0, 0.0).astype(BF16)
    fin[...] = jnp.zeros_like(fin)

    for copy in sent1:
        copy.wait_recv()

    @pl.loop(0, TILES)
    def _(c):
        lanes = pl.ds(pl.multiple_of(c * LANE, LANE), LANE)
        blocks = [rx[g, :, lanes].astype(F32) for g in range(GROUPS)]
        span = 1
        while span < GROUPS:
            for g in range(GROUPS):
                if not g & span:
                    a, b = blocks[g], blocks[g + span]
                    blocks[g], blocks[g + span] = a + b, a - b
            span *= 2
        mixed[:, lanes] = jnp.concatenate(blocks, axis=0).astype(BF16)

    loads[2].wait()

    def turned(start, wide):
        lanes = pl.ds(start, wide)
        y = jnp.dot(mixed[...], turn_v[:, lanes], preferred_element_type=F32)
        tx[:, :, lanes] = y.reshape(GROUPS, TOK // GROUPS, wide).astype(BF16)

    @pl.loop(0, PAIRS - 1)
    def _(c):
        turned(pl.multiple_of(c * WIDE, WIDE), WIDE)

    turned((PAIRS - 1) * WIDE, LANE)
    sent2 = send(tx, rr, s2, r2)
    rr[me] = tx[me]

    @pl.loop(first_rows, TILES)
    def _(r):
        unpack(r)

    loads[3].wait()
    loads[4].wait()
    for copy in sent2:
        copy.wait_recv()

    @pl.loop(0, TILES)
    def _(c):
        lanes = pl.ds(pl.multiple_of(c * LANE, LANE), LANE)
        lhs[:, lanes] = rr[:, :, lanes].astype(F32).reshape(TOK, LANE).astype(BF16)

    across = (x + 1 - 2 * (x % 2), 3 - x)
    half = ((x + 1) // 2 % 2, x // 2)
    mine = (x // 2, x % 2)
    place = ((0, 2, 3, 1), (0, 1, 2, 3))

    def first(p, t):
        return pltpu.make_async_remote_copy(
            src_ref=part.at[p, t, pl.ds(2 * (1 - half[t]), 2)], dst_ref=in1.at[p, t],
            send_sem=sx1.at[p, t], recv_sem=rx1.at[p, t],
            device_id={"tensor": z * NX + across[t]}, device_id_type=MESH,
        )

    def second(p, t):
        return pltpu.make_async_remote_copy(
            src_ref=out2.at[p, t], dst_ref=in2.at[p, t], send_sem=sx2.at[p, t], recv_sem=rx2.at[p, t],
            device_id={"tensor": z * NX + across[1 - t]}, device_id_type=MESH,
        )

    def third(p, dz, tiles):
        there = (z + dz) % NZ
        return pltpu.make_async_remote_copy(
            src_ref=summed.at[p, there, pl.ds(0, tiles)], dst_ref=in3.at[p, dz - 1, pl.ds(0, tiles)],
            send_sem=sz.at[p, dz - 1], recv_sem=rz.at[p, dz - 1],
            device_id={"tensor": there * NX + x}, device_id_type=MESH,
        )

    def multiply(p, tiles):
        for k in range(DIGITS):
            y = jnp.dot(lhs[...], codes[p * DIGITS + k, :, : tiles * LANE], preferred_element_type=F32)
            y = y.reshape(NZ, NX, TOK // GROUPS, tiles * LANE)
            for t in range(tiles):
                for xx in range(NX):
                    part[p, t, place[t][xx], :, :, k * LANE : (k + 1) * LANE] = y[
                        :, xx, :, t * LANE : (t + 1) * LANE
                    ].astype(BF16)
        for t in range(tiles):
            first(p, t).start()

    def halve(p, tiles):
        for t in range(tiles):
            first(p, t).wait_recv()
            other = 1 - mine[t]
            out2[p, t] = (
                part[p, t, 2 * half[t] + other].astype(F32) + in1[p, t, other].astype(F32)
            ).astype(BF16)
            second(p, t).start()

    def spread(p, tiles):
        for t in range(tiles):
            second(p, t).wait_recv()
            total = part[p, t, 2 * half[t] + mine[t]].astype(F32) + in1[p, t, mine[t]].astype(F32)
            summed[p, :, t] = (total + in2[p, t].astype(F32)).astype(BF16)
        for dz in (2, 1, 3):
            third(p, dz, tiles).start()

    def gather(p, tiles):
        for dz in (2, 1, 3):
            third(p, dz, tiles).wait_recv()
        total = summed[p, z, :tiles].astype(F32)
        for n in range(NZ - 1):
            total = total + in3[p, n, :tiles].astype(F32)
        total = total.reshape(tiles * 8, BLOCK)
        if tiles == 1:
            total = jnp.concatenate([total, jnp.zeros_like(total)], axis=0)
        high = total.astype(BF16)
        rows = pl.ds(pl.multiple_of(p * 16, 16), 16)
        fin[0, rows, :] = high
        fin[1, rows, :] = (total - high.astype(F32)).astype(BF16)

    stages = (multiply, halve, spread, gather)
    lags = (0, 2, 4, 6)
    last = PAIRS - 1
    for p in range(lags[-1]):
        for stage, lag in zip(stages, lags):
            if p >= lag:
                stage(p - lag, 2)

    @pl.loop(lags[-1], last)
    def _(p):
        for stage, lag in zip(stages, lags):
            stage(p - lag, 2)

    for p in range(last, last + lags[-1] + 1):
        for stage, lag in zip(stages, lags):
            if p - lag <= last:
                stage(p - lag, 2 if p - lag < last else 1)

    y = jnp.dot(fin[...].reshape(2 * PAIRS * 16, BLOCK), perm[...], preferred_element_type=F32)
    y = y[: PAIRS * 16] + y[PAIRS * 16 :]
    for t in range(TILES):
        lanes = pl.ds(t * BLOCK, BLOCK)
        out[:, lanes] = (
            res_v[:, lanes].astype(F32) + y[8 * t : 8 * t + 8] * scl_v[lanes].reshape(1, BLOCK)
        ).astype(BF16)

    for copy in sent1 + sent2:
        copy.wait_send()

    @pl.loop(0, last)
    def _(p):
        for t in range(2):
            first(p, t).wait_send()
            second(p, t).wait_send()
        for dz in (1, 2, 3):
            third(p, dz, 2).wait_send()

    first(last, 0).wait_send()
    second(last, 0).wait_send()
    for dz in (1, 2, 3):
        third(last, dz, 1).wait_send()


def shards(hidden, residual, sign_bits, packed, scales):
    width = BLOCK * TILES
    dma = pltpu.SemaphoreType.DMA
    vmem = pltpu.VMEM
    tok = TOK // GROUPS
    return pl.pallas_call(
        kernel,
        out_shape=jax.ShapeDtypeStruct((tok, width), BF16),
        in_specs=[pl.BlockSpec(memory_space=pl.ANY)] * 6,
        out_specs=pl.BlockSpec(memory_space=pltpu.VMEM),
        scratch_shapes=[
            vmem((GROUPS, tok, ROW), BF16),
            vmem((tok, width), BF16),
            vmem((ROW,), jnp.int32),
            vmem((width,), F32),
            vmem((ROW, ROW), BF16),
            vmem((SLOTS, LANE, ROW), F32),
            vmem((PAIRS * DIGITS, ROW, WIDE), BF16),
            vmem((BLOCK, BLOCK), BF16),
            vmem((GROUPS, tok, ROW), BF16),
            vmem((TOK, ROW), BF16),
            vmem((GROUPS, tok, ROW), BF16),
            vmem((GROUPS, tok, ROW), BF16),
            vmem((TOK, ROW), BF16),
            vmem((PAIRS, 2, NX, NZ, tok, BLOCK), BF16),
            vmem((PAIRS, 2, 2, NZ, tok, BLOCK), BF16),
            vmem((PAIRS, 2, NZ, tok, BLOCK), BF16),
            vmem((PAIRS, 2, NZ, tok, BLOCK), BF16),
            vmem((PAIRS, NZ, 2, tok, BLOCK), BF16),
            vmem((PAIRS, NZ - 1, 2, tok, BLOCK), BF16),
            vmem((2, PAIRS * 16, BLOCK), BF16),
            dma((5,)),
            dma((SLOTS,)),
            dma((GROUPS,)),
            dma((GROUPS,)),
            dma((GROUPS,)),
            dma((GROUPS,)),
            dma((PAIRS, 2)),
            dma((PAIRS, 2)),
            dma((PAIRS, 2)),
            dma((PAIRS, 2)),
            dma((PAIRS, NZ - 1)),
            dma((PAIRS, NZ - 1)),
        ],
        compiler_params=pltpu.CompilerParams(
            collective_id=0, has_side_effects=True, vmem_limit_bytes=60 * 1024 * 1024
        ),
        cost_estimate=pl.CostEstimate(flops=4_300_000_000, bytes_accessed=17_000_000, transcendentals=0),
    )(
        hidden.reshape(GROUPS, tok, ROW),
        residual,
        sign_bits,
        packed,
        scales,
        jnp.asarray(turn_table()),
    )


def solution(mesh):
    return jax.shard_map(
        shards,
        mesh=mesh,
        in_specs=(
            P("dp", "tensor"),
            P(("dp", "tensor"), None),
            P("tensor"),
            P("tensor", None),
            P(),
        ),
        out_specs=P(("dp", "tensor"), None),
        check_vma=False,
    )
```

```python
import math

import jax
import jax.numpy as jnp
import numpy as np
from jax import lax
from jax.experimental import pallas as pl
from jax.experimental.pallas import tpu as pltpu
from jax.sharding import PartitionSpec as P

WALSH = 2048
ODD = 13
GROUPS = 16
NX = 4
NZ = 4
TOK = 128
ROW = 1664
DIGITS = 5
LANE = 128
SUB = 8
WIDE = 2 * LANE
PAIRS = 7
TILES = 13
BLOCK = DIGITS * LANE
SLOTS = 4
HALVES = 2
NZS = NZ // HALVES
HALF_TOK = TOK // HALVES
QUADS = 4
START = (0, 7 * LANE)
WIDTH = (7 * LANE, 6 * LANE)
LAGS = (0, 2, 4, 7)
MESH = pl.DeviceIdType.MESH
F32 = jnp.float32
BF16 = jnp.bfloat16


def turn_table():
    local = ROW // ODD
    ids = np.arange(local)
    both = ids[:, None] & ids[None, :]
    parity = np.zeros_like(both)
    for bit in range(local.bit_length() - 1):
        parity ^= (both >> bit) & 1
    walsh = 1.0 - 2.0 * parity
    k = np.arange(ODD)[:, None]
    b = np.arange(ODD)[None, :]
    cosine = np.where(k == 0, math.sqrt(0.5), 1.0) * math.sqrt(2.0 / ODD)
    cosine = cosine * np.cos(math.pi * (2.0 * b + 1.0) * k / (2.0 * ODD))
    return (np.kron(walsh, cosine.T) / math.sqrt(WALSH)).astype(jnp.bfloat16)


OFFSETS = [(dz, dx) for dz in (2, 1, 3, 0) for dx in (2, 1, 3, 0) if dz or dx]


def kernel(
    hid, res, sgn, packed, scl, turn, out,
    hid_v, res_v, sgn_v, scl_v, turn_v, words, codes, perm,
    rx, tx, rr, mixed, lhs, part, in1, out2, in2, summed, in3, fin,
    load_sem, word_sem, s1, r1, s2, r2, sx1, rx1, sx2, rx2, sz, rz,
):
    me = lax.axis_index("tensor")
    z, x = me // NX, me % NX
    loads = []
    for n, (src, dst) in enumerate(
        ((hid, hid_v), (sgn, sgn_v), (turn, turn_v), (res, res_v), (scl, scl_v))
    ):
        loads.append(pltpu.make_async_copy(src, dst, load_sem.at[n]))

    def word_copy(r, slot):
        return pltpu.make_async_copy(
            packed.at[pl.ds(pl.multiple_of(r * LANE, LANE), LANE)], words.at[slot], word_sem.at[slot]
        )

    loads[0].start()
    loads[1].start()
    barrier = pltpu.get_barrier_semaphore()
    for dz, dx in OFFSETS:
        peer = (z + dz) % NZ * NX + (x + dx) % NX
        pl.semaphore_signal(barrier, inc=1, device_id={"tensor": peer}, device_id_type=MESH)
    for r in range(SLOTS):
        word_copy(r, r).start()
    for n in (2, 3, 4):
        loads[n].start()

    loads[0].wait()
    loads[1].wait()

    @pl.loop(0, TILES)
    def _(c):
        lanes = pl.ds(pl.multiple_of(c * LANE, LANE), LANE)
        flips = (2 * sgn_v[lanes] - 1).astype(F32).reshape(1, LANE)
        hid_v[:, :, lanes] = (hid_v[:, :, lanes].astype(F32) * flips).astype(BF16)

    def by_parity(run):
        for parity in range(2):

            @pl.when(x % 2 == parity)
            def _():
                run(parity)

    def z_of(h, n):
        return 3 * n if h == 0 else 1 + n

    def in_half(h):
        return (z % 3 == 0) if h == 0 else (z % 3 != 0)

    def place_in_half(h):
        return z // 3 if h == 0 else z - 1

    def group(h, number):
        return z_of(h, number // 2 // NX) * NX + number // 2 % NX

    def scatter(h, dz, dx, parity):
        peer = (z + dz) % NZ * NX + (x + dx) % NX
        theirs = (parity + dx) % 2
        off = dz * NX + dx
        return pltpu.make_async_remote_copy(
            src_ref=hid_v.at[group(h, peer), :, pl.ds(START[theirs], WIDTH[theirs])],
            dst_ref=rx.at[h, me, :, pl.ds(0, WIDTH[theirs])],
            send_sem=s1.at[h, off], recv_sem=r1.at[h, off],
            device_id={"tensor": peer}, device_id_type=MESH,
        )

    def scattered(h, dz, dx, parity):
        source = (z + NZ - dz) % NZ * NX + (x + NX - dx) % NX
        off = dz * NX + dx
        there = rx.at[h, source, :, pl.ds(0, WIDTH[parity])]
        return pltpu.make_async_remote_copy(
            src_ref=there, dst_ref=there, send_sem=s1.at[h, off], recv_sem=r1.at[h, off],
            device_id={"tensor": source}, device_id_type=MESH,
        )

    def back(h, dz, dx, parity):
        peer = (z + dz) % NZ * NX + (x + dx) % NX
        off = dz * NX + dx
        return pltpu.make_async_remote_copy(
            src_ref=tx.at[h, peer, :, pl.ds(0, WIDTH[parity])],
            dst_ref=rr.at[h, me // 2, :, pl.ds(START[parity], WIDTH[parity])],
            send_sem=s2.at[h, off], recv_sem=r2.at[h, off],
            device_id={"tensor": peer}, device_id_type=MESH,
        )

    def came_back(h, dz, dx, parity):
        source = (z + NZ - dz) % NZ * NX + (x + NX - dx) % NX
        theirs = (parity + dx) % 2
        off = dz * NX + dx
        there = rr.at[h, source // 2, :, pl.ds(START[theirs], WIDTH[theirs])]
        return pltpu.make_async_remote_copy(
            src_ref=there, dst_ref=there, send_sem=s2.at[h, off], recv_sem=r2.at[h, off],
            device_id={"tensor": source}, device_id_type=MESH,
        )

    def send_out(h):
        def run(parity):
            for dz, dx in OFFSETS:
                scatter(h, dz, dx, parity).start()
            rx[h, me, :, : WIDTH[parity]] = hid_v[
                group(h, me), :, START[parity] : START[parity] + WIDTH[parity]
            ]

        by_parity(run)

    def mix(h):
        def wait(parity):
            for dz, dx in OFFSETS:
                scattered(h, dz, dx, parity).wait_recv()

        by_parity(wait)

        def mix_tile(c):
            lanes = pl.ds(c * LANE, LANE)
            blocks = [rx[h, g, :, lanes].astype(F32) for g in range(GROUPS)]
            span = 1
            while span < GROUPS:
                for g in range(GROUPS):
                    if not g & span:
                        a, b = blocks[g], blocks[g + span]
                        blocks[g], blocks[g + span] = a + b, a - b
                span *= 2
            for g in range(GROUPS):
                tx[h, g, :, lanes] = blocks[g].astype(BF16)

        for c in range(6):
            mix_tile(c)

        @pl.when(x % 2 == 0)
        def _():
            mix_tile(6)

        def run(parity):
            for dz, dx in OFFSETS:
                back(h, dz, dx, parity).start()
            rr[h, me // 2, :, START[parity] : START[parity] + WIDTH[parity]] = tx[h, me, :, : WIDTH[parity]]

        by_parity(run)

    def local_turn(h):
        def wait(parity):
            for dz, dx in OFFSETS:
                came_back(h, dz, dx, parity).wait_recv()

        by_parity(wait)

        for c in range(TILES):
            lanes = pl.ds(c * LANE, LANE)
            mixed[:, lanes] = rr[h, :, :, lanes].astype(F32).reshape(HALF_TOK, LANE).astype(BF16)

        def turned(start, wide):
            lanes = pl.ds(start, wide)
            y = jnp.dot(mixed[...], turn_v[:, lanes], preferred_element_type=F32)
            lhs[h, :, lanes] = y.astype(BF16)

        for c in range(PAIRS - 1):
            turned(c * WIDE, WIDE)

        turned((PAIRS - 1) * WIDE, LANE)

    def unpack(r):
        slot = r % SLOTS
        word_copy(r, slot).wait()
        rows = pl.ds(pl.multiple_of(r * LANE, LANE), LANE)
        for p in range(PAIRS):
            wide = WIDE if p < PAIRS - 1 else LANE
            word = words[slot, :, p * WIDE : p * WIDE + wide].astype(jnp.int32) ^ 0x88888
            for k in range(DIGITS):
                digit = (word << (28 - 4 * k)) >> 28
                codes[p * DIGITS + k, rows, :wide] = digit.astype(F32).astype(BF16)

        @pl.when(r + SLOTS < TILES)
        def _():
            word_copy(r + SLOTS, slot).start()

    pl.semaphore_wait(barrier, GROUPS - 1)
    send_out(0)
    stops = (0, 5, 9, TILES)

    @pl.loop(stops[0], stops[1])
    def _(r):
        unpack(r)

    mix(0)

    @pl.loop(stops[1], stops[2])
    def _(r):
        unpack(r)


    @pl.loop(stops[2], stops[3])
    def _(r):
        unpack(r)

    rows = lax.broadcasted_iota(jnp.int32, (BLOCK, BLOCK), 0)
    cols = lax.broadcasted_iota(jnp.int32, (BLOCK, BLOCK), 1)
    perm[...] = jnp.where((rows & (LANE - 1)) * DIGITS + (rows >> 7) == cols, 1.0, 0.0).astype(BF16)
    fin[...] = jnp.zeros_like(fin)
    for n in (2, 3, 4):
        loads[n].wait()

    across = (x + 1 - 2 * (x % 2), 3 - x)
    half = ((x + 1) // 2 % 2, x // 2)
    mine = (x // 2, x % 2)
    place = ((0, 2, 3, 1), (0, 1, 2, 3))

    def shape(h, c):
        return ((0, 1), 2) if c < QUADS - 1 else ((h,), 1)

    def first(h, c, t, pairs):
        return pltpu.make_async_remote_copy(
            src_ref=part.at[h, c, t, pl.ds(2 * (1 - half[t]), 2), pl.ds(0, pairs)],
            dst_ref=in1.at[h, c, t, :, pl.ds(0, pairs)],
            send_sem=sx1.at[h, c, t], recv_sem=rx1.at[h, c, t],
            device_id={"tensor": z * NX + across[t]}, device_id_type=MESH,
        )

    def second(h, c, t, pairs):
        return pltpu.make_async_remote_copy(
            src_ref=out2.at[h, c, t, pl.ds(0, pairs)], dst_ref=in2.at[h, c, t, pl.ds(0, pairs)],
            send_sem=sx2.at[h, c, t], recv_sem=rx2.at[h, c, t],
            device_id={"tensor": z * NX + across[1 - t]}, device_id_type=MESH,
        )

    def third(h, c, n):
        kinds, pairs = shape(h, c)
        there = z_of(h, n)
        off = (there + NZ - z) % NZ
        which = (pl.ds(kinds[0], len(kinds)), pl.ds(0, pairs))
        return off, pltpu.make_async_remote_copy(
            src_ref=summed.at[h, c, n, *which], dst_ref=in3.at[h, c, (off + NZ - 1) % NZ, *which],
            send_sem=sz.at[h, c, n], recv_sem=rz.at[h, c, (off + NZ - 1) % NZ],
            device_id={"tensor": there * NX + x}, device_id_type=MESH,
        )

    def third_in(h, c, off):
        kinds, pairs = shape(h, c)
        which = (pl.ds(kinds[0], len(kinds)), pl.ds(0, pairs))
        there = in3.at[h, c, off - 1, *which]
        return pltpu.make_async_remote_copy(
            src_ref=there, dst_ref=there, send_sem=sz.at[h, c, 0], recv_sem=rz.at[h, c, off - 1],
            device_id={"tensor": (z + NZ - off) % NZ * NX + x}, device_id_type=MESH,
        )

    def multiply(h, c):
        kinds, pairs = shape(h, c)

        for k in range(DIGITS):
            lanes = pl.ds(k * LANE, LANE)
            for n in range(pairs):
                wide = LANE * len(kinds)
                code = codes[(2 * c + n) * DIGITS + k, :, :wide]
                y = jnp.dot(lhs[h], code, preferred_element_type=F32)
                y = y.reshape(NZS, NX, SUB, wide)
                for i, t in enumerate(kinds):
                    for xx in range(NX):
                        part[h, c, t, place[t][xx], n, :, :, lanes] = y[
                            :, xx, :, i * LANE : (i + 1) * LANE
                        ].astype(BF16)

        for t in kinds:
            first(h, c, t, pairs).start()

    def halve(h, c):
        kinds, pairs = shape(h, c)
        for t in kinds:
            first(h, c, t, pairs).wait_recv()
            other = 1 - mine[t]
            total = part[h, c, t, 2 * half[t] + other, :pairs].astype(F32)
            out2[h, c, t, :pairs] = (total + in1[h, c, t, other, :pairs].astype(F32)).astype(BF16)
            second(h, c, t, pairs).start()

    def spread(h, c):
        kinds, pairs = shape(h, c)
        for t in kinds:
            second(h, c, t, pairs).wait_recv()
            total = part[h, c, t, 2 * half[t] + mine[t], :pairs].astype(F32)
            total = total + in1[h, c, t, mine[t], :pairs].astype(F32)
            total = (total + in2[h, c, t, :pairs].astype(F32)).astype(BF16)
            for n in range(NZS):
                summed[h, c, n, t, :pairs] = total[:, n]
        for n in range(NZS):
            off, copy = third(h, c, n)

            @pl.when(off != 0)
            def _():
                copy.start()

    def gather(h, c):
        kinds, pairs = shape(h, c)
        n = place_in_half(h)

        @pl.when(in_half(h))
        def _():
            for off in range(1, NZ):
                third_in(h, c, off).wait_recv()
            for q in range(pairs):
                totals = []
                for t in kinds:
                    total = summed[h, c, n, t, q].astype(F32)
                    for m in range(NZ - 1):
                        total = total + in3[h, c, m, t, q].astype(F32)
                    totals.append(total)
                if len(totals) == 1:
                    totals.append(jnp.zeros_like(totals[0]))
                total = jnp.concatenate(totals, axis=0)
                high = total.astype(BF16)
                rows = pl.ds((2 * c + q) * 16, 16)
                fin[0, rows, :] = high
                fin[1, rows, :] = (total - high.astype(F32)).astype(BF16)

    last = QUADS - 1
    chunks = [(0, last)] + [(0, c) for c in range(last)] + [(1, c) for c in range(QUADS)]
    stages = (multiply, halve, spread, gather)
    for step in range(len(chunks) + LAGS[-1]):
        if step < len(chunks) and (step == 0 or chunks[step][0] != chunks[step - 1][0]):
            local_turn(chunks[step][0])
            if step == 0:
                send_out(1)
        if step == 3:
            mix(1)
        for stage, lag in zip(stages, LAGS):
            if 0 <= step - lag < len(chunks):
                stage(*chunks[step - lag])

    y = jnp.dot(fin[...].reshape(2 * PAIRS * 16, BLOCK), perm[...], preferred_element_type=F32)
    y = y[: PAIRS * 16] + y[PAIRS * 16 :]
    for t in range(TILES):
        lanes = pl.ds(t * BLOCK, BLOCK)
        out[:, lanes] = (
            res_v[:, lanes].astype(F32) + y[8 * t : 8 * t + 8] * scl_v[lanes].reshape(1, BLOCK)
        ).astype(BF16)

    def drain(parity):
        for h in range(HALVES):
            for dz, dx in OFFSETS:
                scatter(h, dz, dx, parity).wait_send()
                back(h, dz, dx, parity).wait_send()

    by_parity(drain)
    for h, c in chunks:
        kinds, pairs = shape(h, c)
        for t in kinds:
            first(h, c, t, pairs).wait_send()
            second(h, c, t, pairs).wait_send()
        for n in range(NZS):
            off, copy = third(h, c, n)

            @pl.when(off != 0)
            def _():
                copy.wait_send()


def shards(hidden, residual, sign_bits, packed, scales):
    width = BLOCK * TILES
    dma = pltpu.SemaphoreType.DMA
    vmem = pltpu.VMEM
    tok = TOK // GROUPS
    return pl.pallas_call(
        kernel,
        out_shape=jax.ShapeDtypeStruct((tok, width), BF16),
        in_specs=[pl.BlockSpec(memory_space=pl.ANY)] * 6,
        out_specs=pl.BlockSpec(memory_space=pltpu.VMEM),
        scratch_shapes=[
            vmem((GROUPS, tok, ROW), BF16),
            vmem((tok, width), BF16),
            vmem((ROW,), jnp.int32),
            vmem((width,), F32),
            vmem((ROW, ROW), BF16),
            vmem((SLOTS, LANE, ROW), F32),
            vmem((PAIRS * DIGITS, ROW, WIDE), BF16),
            vmem((BLOCK, BLOCK), BF16),
            vmem((HALVES, GROUPS, tok, WIDTH[0]), BF16),
            vmem((HALVES, GROUPS, tok, WIDTH[0]), BF16),
            vmem((HALVES, GROUPS // 2, tok, ROW), BF16),
            vmem((HALF_TOK, ROW), BF16),
            vmem((HALVES, HALF_TOK, ROW), BF16),
            vmem((HALVES, QUADS, 2, NX, 2, NZS, tok, BLOCK), BF16),
            vmem((HALVES, QUADS, 2, 2, 2, NZS, tok, BLOCK), BF16),
            vmem((HALVES, QUADS, 2, 2, NZS, tok, BLOCK), BF16),
            vmem((HALVES, QUADS, 2, 2, NZS, tok, BLOCK), BF16),
            vmem((HALVES, QUADS, NZS, 2, 2, tok, BLOCK), BF16),
            vmem((HALVES, QUADS, NZ - 1, 2, 2, tok, BLOCK), BF16),
            vmem((2, PAIRS * 16, BLOCK), BF16),
            dma((5,)),
            dma((SLOTS,)),
            dma((HALVES, GROUPS)),
            dma((HALVES, GROUPS)),
            dma((HALVES, GROUPS)),
            dma((HALVES, GROUPS)),
            dma((HALVES, QUADS, 2)),
            dma((HALVES, QUADS, 2)),
            dma((HALVES, QUADS, 2)),
            dma((HALVES, QUADS, 2)),
            dma((HALVES, QUADS, NZS)),
            dma((HALVES, QUADS, NZ - 1)),
        ],
        compiler_params=pltpu.CompilerParams(
            collective_id=0, has_side_effects=True, vmem_limit_bytes=60 * 1024 * 1024
        ),
        cost_estimate=pl.CostEstimate(flops=4_300_000_000, bytes_accessed=17_000_000, transcendentals=0),
    )(
        hidden.reshape(GROUPS, tok, ROW),
        residual,
        sign_bits,
        packed,
        scales,
        jnp.asarray(turn_table()),
    )


def solution(mesh):
    return jax.shard_map(
        shards,
        mesh=mesh,
        in_specs=(
            P("dp", "tensor"),
            P(("dp", "tensor"), None),
            P("tensor"),
            P("tensor", None),
            P(),
        ),
        out_specs=P(("dp", "tensor"), None),
        check_vma=False,
    )
```

```python
import math

import jax
import jax.numpy as jnp
import numpy as np
from jax import lax
from jax.experimental import pallas as pl
from jax.experimental.pallas import tpu as pltpu
from jax.sharding import PartitionSpec as P

WALSH = 2048
ODD = 13
GROUPS = 16
NX = 4
NZ = 4
TOK = 128
ROW = 1664
DIGITS = 5
LANE = 128
SUB = 8
WIDE = 2 * LANE
PAIRS = 7
TILES = 13
BLOCK = DIGITS * LANE
SLOTS = 4
HALVES = 2
NZS = NZ // HALVES
HALF_TOK = TOK // HALVES
QUADS = 4
START = (0, 7 * LANE)
WIDTH = (7 * LANE, 6 * LANE)
LAGS = (0, 2, 4, 7)
MESH = pl.DeviceIdType.MESH
F32 = jnp.float32
BF16 = jnp.bfloat16


def turn_table():
    local = ROW // ODD
    ids = np.arange(local)
    both = ids[:, None] & ids[None, :]
    parity = np.zeros_like(both)
    for bit in range(local.bit_length() - 1):
        parity ^= (both >> bit) & 1
    walsh = 1.0 - 2.0 * parity
    k = np.arange(ODD)[:, None]
    b = np.arange(ODD)[None, :]
    cosine = np.where(k == 0, math.sqrt(0.5), 1.0) * math.sqrt(2.0 / ODD)
    cosine = cosine * np.cos(math.pi * (2.0 * b + 1.0) * k / (2.0 * ODD))
    return (np.kron(walsh, cosine.T) / math.sqrt(WALSH)).astype(jnp.bfloat16)


OFFSETS = [(dz, dx) for dz in (2, 1, 3, 0) for dx in (2, 1, 3, 0) if dz or dx]


def kernel(
    hid, res, sgn, packed, scl, turn, out,
    hid_v, res_v, sgn_v, scl_v, turn_v, words, codes, perm,
    rx, tx, rr, mixed, lhs, part, in1, out2, in2, summed, in3, fin,
    load_sem, word_sem, s1, r1, s2, r2, sx1, rx1, sx2, rx2, sz, rz,
):
    me = lax.axis_index("tensor")
    z, x = me // NX, me % NX
    loads = []
    for n, (src, dst) in enumerate(
        ((hid, hid_v), (sgn, sgn_v), (turn, turn_v), (res, res_v), (scl, scl_v))
    ):
        loads.append(pltpu.make_async_copy(src, dst, load_sem.at[n]))

    def word_copy(r, slot):
        return pltpu.make_async_copy(
            packed.at[pl.ds(pl.multiple_of(r * LANE, LANE), LANE)], words.at[slot], word_sem.at[slot]
        )

    loads[0].start()
    loads[1].start()
    barrier = pltpu.get_barrier_semaphore()
    for dz, dx in OFFSETS:
        peer = (z + dz) % NZ * NX + (x + dx) % NX
        pl.semaphore_signal(barrier, inc=1, device_id={"tensor": peer}, device_id_type=MESH)
    for r in range(SLOTS):
        word_copy(r, r).start()
    for n in (2, 3, 4):
        loads[n].start()

    loads[0].wait()
    loads[1].wait()

    @pl.loop(0, TILES)
    def _(c):
        lanes = pl.ds(pl.multiple_of(c * LANE, LANE), LANE)
        flips = (2 * sgn_v[lanes] - 1).astype(F32).reshape(1, LANE)
        hid_v[:, :, lanes] = (hid_v[:, :, lanes].astype(F32) * flips).astype(BF16)

    def by_parity(run):
        for parity in range(2):

            @pl.when(x % 2 == parity)
            def _():
                run(parity)

    def z_of(h, n):
        return 3 * n if h == 0 else 1 + n

    def in_half(h):
        return (z % 3 == 0) if h == 0 else (z % 3 != 0)

    def place_in_half(h):
        return z // 3 if h == 0 else z - 1

    def group(h, number):
        return z_of(h, number // 2 // NX) * NX + number // 2 % NX

    def scatter(h, dz, dx, parity):
        peer = (z + dz) % NZ * NX + (x + dx) % NX
        theirs = (parity + dx) % 2
        off = dz * NX + dx
        return pltpu.make_async_remote_copy(
            src_ref=hid_v.at[group(h, peer), :, pl.ds(START[theirs], WIDTH[theirs])],
            dst_ref=rx.at[h, me, :, pl.ds(0, WIDTH[theirs])],
            send_sem=s1.at[h, off], recv_sem=r1.at[h, off],
            device_id={"tensor": peer}, device_id_type=MESH,
        )

    def scattered(h, dz, dx, parity):
        source = (z + NZ - dz) % NZ * NX + (x + NX - dx) % NX
        off = dz * NX + dx
        there = rx.at[h, source, :, pl.ds(0, WIDTH[parity])]
        return pltpu.make_async_remote_copy(
            src_ref=there, dst_ref=there, send_sem=s1.at[h, off], recv_sem=r1.at[h, off],
            device_id={"tensor": source}, device_id_type=MESH,
        )

    def back(h, dz, dx, parity):
        peer = (z + dz) % NZ * NX + (x + dx) % NX
        off = dz * NX + dx
        return pltpu.make_async_remote_copy(
            src_ref=tx.at[h, peer, :, pl.ds(0, WIDTH[parity])],
            dst_ref=rr.at[h, me // 2, :, pl.ds(START[parity], WIDTH[parity])],
            send_sem=s2.at[h, off], recv_sem=r2.at[h, off],
            device_id={"tensor": peer}, device_id_type=MESH,
        )

    def came_back(h, dz, dx, parity):
        source = (z + NZ - dz) % NZ * NX + (x + NX - dx) % NX
        theirs = (parity + dx) % 2
        off = dz * NX + dx
        there = rr.at[h, source // 2, :, pl.ds(START[theirs], WIDTH[theirs])]
        return pltpu.make_async_remote_copy(
            src_ref=there, dst_ref=there, send_sem=s2.at[h, off], recv_sem=r2.at[h, off],
            device_id={"tensor": source}, device_id_type=MESH,
        )

    def send_out(h):
        def run(parity):
            for dz, dx in OFFSETS:
                scatter(h, dz, dx, parity).start()
            rx[h, me, :, : WIDTH[parity]] = hid_v[
                group(h, me), :, START[parity] : START[parity] + WIDTH[parity]
            ]

        by_parity(run)

    def mix(h):
        def wait(parity):
            for dz, dx in OFFSETS:
                scattered(h, dz, dx, parity).wait_recv()

        by_parity(wait)

        def mix_tile(c):
            lanes = pl.ds(c * LANE, LANE)
            blocks = [rx[h, g, :, lanes].astype(F32) for g in range(GROUPS)]
            span = 1
            while span < GROUPS:
                for g in range(GROUPS):
                    if not g & span:
                        a, b = blocks[g], blocks[g + span]
                        blocks[g], blocks[g + span] = a + b, a - b
                span *= 2
            for g in range(GROUPS):
                tx[h, g, :, lanes] = blocks[g].astype(BF16)

        for c in range(6):
            mix_tile(c)

        @pl.when(x % 2 == 0)
        def _():
            mix_tile(6)

        def run(parity):
            for dz, dx in OFFSETS:
                back(h, dz, dx, parity).start()
            rr[h, me // 2, :, START[parity] : START[parity] + WIDTH[parity]] = tx[h, me, :, : WIDTH[parity]]

        by_parity(run)

    def local_turn(h):
        def wait(parity):
            for dz, dx in OFFSETS:
                came_back(h, dz, dx, parity).wait_recv()

        by_parity(wait)
        if h == 0:
            send_out(1)

        for c in range(TILES):
            lanes = pl.ds(c * LANE, LANE)
            mixed[:, lanes] = rr[h, :, :, lanes].astype(F32).reshape(HALF_TOK, LANE).astype(BF16)

        def turned(start, wide):
            lanes = pl.ds(start, wide)
            y = jnp.dot(mixed[...], turn_v[:, lanes], preferred_element_type=F32)
            lhs[h, :, lanes] = y.astype(BF16)

        for c in range(PAIRS - 1):
            turned(c * WIDE, WIDE)

        turned((PAIRS - 1) * WIDE, LANE)

    def unpack(r):
        slot = r % SLOTS
        word_copy(r, slot).wait()
        rows = pl.ds(pl.multiple_of(r * LANE, LANE), LANE)
        for p in range(PAIRS):
            wide = WIDE if p < PAIRS - 1 else LANE
            word = words[slot, :, p * WIDE : p * WIDE + wide].astype(jnp.int32) ^ 0x88888
            for k in range(DIGITS):
                digit = (word << (28 - 4 * k)) >> 28
                codes[p * DIGITS + k, rows, :wide] = digit.astype(F32).astype(BF16)

        @pl.when(r + SLOTS < TILES)
        def _():
            word_copy(r + SLOTS, slot).start()

    pl.semaphore_wait(barrier, GROUPS - 1)
    send_out(0)
    stops = (0, 5, 9, TILES)

    @pl.loop(stops[0], stops[1])
    def _(r):
        unpack(r)

    mix(0)

    @pl.loop(stops[1], stops[2])
    def _(r):
        unpack(r)


    @pl.loop(stops[2], stops[3])
    def _(r):
        unpack(r)

    rows = lax.broadcasted_iota(jnp.int32, (BLOCK, BLOCK), 0)
    cols = lax.broadcasted_iota(jnp.int32, (BLOCK, BLOCK), 1)
    perm[...] = jnp.where((rows & (LANE - 1)) * DIGITS + (rows >> 7) == cols, 1.0, 0.0).astype(BF16)
    fin[...] = jnp.zeros_like(fin)
    for n in (2, 3, 4):
        loads[n].wait()

    across = (x + 1 - 2 * (x % 2), 3 - x)
    half = ((x + 1) // 2 % 2, x // 2)
    mine = (x // 2, x % 2)
    place = ((0, 2, 3, 1), (0, 1, 2, 3))

    def shape(h, c):
        return ((0, 1), 2) if c < QUADS - 1 else ((h,), 1)

    def first(h, c, t, pairs):
        return pltpu.make_async_remote_copy(
            src_ref=part.at[h, c, t, pl.ds(2 * (1 - half[t]), 2), pl.ds(0, pairs)],
            dst_ref=in1.at[h, c, t, :, pl.ds(0, pairs)],
            send_sem=sx1.at[h, c, t], recv_sem=rx1.at[h, c, t],
            device_id={"tensor": z * NX + across[t]}, device_id_type=MESH,
        )

    def second(h, c, t, pairs):
        return pltpu.make_async_remote_copy(
            src_ref=out2.at[h, c, t, pl.ds(0, pairs)], dst_ref=in2.at[h, c, t, pl.ds(0, pairs)],
            send_sem=sx2.at[h, c, t], recv_sem=rx2.at[h, c, t],
            device_id={"tensor": z * NX + across[1 - t]}, device_id_type=MESH,
        )

    def third(h, c, n):
        kinds, pairs = shape(h, c)
        there = z_of(h, n)
        off = (there + NZ - z) % NZ
        which = (pl.ds(kinds[0], len(kinds)), pl.ds(0, pairs))
        return off, pltpu.make_async_remote_copy(
            src_ref=summed.at[h, c, n, *which], dst_ref=in3.at[h, c, (off + NZ - 1) % NZ, *which],
            send_sem=sz.at[h, c, n], recv_sem=rz.at[h, c, (off + NZ - 1) % NZ],
            device_id={"tensor": there * NX + x}, device_id_type=MESH,
        )

    def third_in(h, c, off):
        kinds, pairs = shape(h, c)
        which = (pl.ds(kinds[0], len(kinds)), pl.ds(0, pairs))
        there = in3.at[h, c, off - 1, *which]
        return pltpu.make_async_remote_copy(
            src_ref=there, dst_ref=there, send_sem=sz.at[h, c, 0], recv_sem=rz.at[h, c, off - 1],
            device_id={"tensor": (z + NZ - off) % NZ * NX + x}, device_id_type=MESH,
        )

    def multiply(h, c):
        kinds, pairs = shape(h, c)

        for k in range(DIGITS):
            lanes = pl.ds(k * LANE, LANE)
            for n in range(pairs):
                wide = LANE * len(kinds)
                code = codes[(2 * c + n) * DIGITS + k, :, :wide]
                y = jnp.dot(lhs[h], code, preferred_element_type=F32)
                y = y.reshape(NZS, NX, SUB, wide)
                for i, t in enumerate(kinds):
                    for xx in range(NX):
                        part[h, c, t, place[t][xx], n, :, :, lanes] = y[
                            :, xx, :, i * LANE : (i + 1) * LANE
                        ].astype(BF16)

        for t in kinds:
            first(h, c, t, pairs).start()

    def halve(h, c):
        kinds, pairs = shape(h, c)
        for t in kinds:
            first(h, c, t, pairs).wait_recv()
            other = 1 - mine[t]
            total = part[h, c, t, 2 * half[t] + other, :pairs].astype(F32)
            out2[h, c, t, :pairs] = (total + in1[h, c, t, other, :pairs].astype(F32)).astype(BF16)
            second(h, c, t, pairs).start()

    def spread(h, c):
        kinds, pairs = shape(h, c)
        for t in kinds:
            second(h, c, t, pairs).wait_recv()
            total = part[h, c, t, 2 * half[t] + mine[t], :pairs].astype(F32)
            total = total + in1[h, c, t, mine[t], :pairs].astype(F32)
            total = (total + in2[h, c, t, :pairs].astype(F32)).astype(BF16)
            for n in range(NZS):
                summed[h, c, n, t, :pairs] = total[:, n]
        for n in range(NZS):
            off, copy = third(h, c, n)

            @pl.when(off != 0)
            def _():
                copy.start()

    def gather(h, c):
        kinds, pairs = shape(h, c)
        n = place_in_half(h)

        @pl.when(in_half(h))
        def _():
            for off in range(1, NZ):
                third_in(h, c, off).wait_recv()
            for q in range(pairs):
                totals = []
                for t in kinds:
                    total = summed[h, c, n, t, q].astype(F32)
                    for m in range(NZ - 1):
                        total = total + in3[h, c, m, t, q].astype(F32)
                    totals.append(total)
                if len(totals) == 1:
                    totals.append(jnp.zeros_like(totals[0]))
                total = jnp.concatenate(totals, axis=0)
                high = total.astype(BF16)
                rows = pl.ds((2 * c + q) * 16, 16)
                fin[0, rows, :] = high
                fin[1, rows, :] = (total - high.astype(F32)).astype(BF16)

    last = QUADS - 1
    chunks = [(0, last)] + [(0, c) for c in range(last)] + [(1, c) for c in range(QUADS)]
    stages = (multiply, halve, spread, gather)
    for step in range(len(chunks) + LAGS[-1]):
        if step < len(chunks) and (step == 0 or chunks[step][0] != chunks[step - 1][0]):
            local_turn(chunks[step][0])
        if step == 2:
            mix(1)
        for stage, lag in zip(stages, LAGS):
            if 0 <= step - lag < len(chunks):
                stage(*chunks[step - lag])

    y = jnp.dot(fin[...].reshape(2 * PAIRS * 16, BLOCK), perm[...], preferred_element_type=F32)
    y = y[: PAIRS * 16] + y[PAIRS * 16 :]
    for t in range(TILES):
        lanes = pl.ds(t * BLOCK, BLOCK)
        out[:, lanes] = (
            res_v[:, lanes].astype(F32) + y[8 * t : 8 * t + 8] * scl_v[lanes].reshape(1, BLOCK)
        ).astype(BF16)

    def drain(parity):
        for h in range(HALVES):
            for dz, dx in OFFSETS:
                scatter(h, dz, dx, parity).wait_send()
                back(h, dz, dx, parity).wait_send()

    by_parity(drain)
    for h, c in chunks:
        kinds, pairs = shape(h, c)
        for t in kinds:
            first(h, c, t, pairs).wait_send()
            second(h, c, t, pairs).wait_send()
        for n in range(NZS):
            off, copy = third(h, c, n)

            @pl.when(off != 0)
            def _():
                copy.wait_send()


def shards(hidden, residual, sign_bits, packed, scales):
    width = BLOCK * TILES
    dma = pltpu.SemaphoreType.DMA
    vmem = pltpu.VMEM
    tok = TOK // GROUPS
    return pl.pallas_call(
        kernel,
        out_shape=jax.ShapeDtypeStruct((tok, width), BF16),
        in_specs=[pl.BlockSpec(memory_space=pl.ANY)] * 6,
        out_specs=pl.BlockSpec(memory_space=pltpu.VMEM),
        scratch_shapes=[
            vmem((GROUPS, tok, ROW), BF16),
            vmem((tok, width), BF16),
            vmem((ROW,), jnp.int32),
            vmem((width,), F32),
            vmem((ROW, ROW), BF16),
            vmem((SLOTS, LANE, ROW), F32),
            vmem((PAIRS * DIGITS, ROW, WIDE), BF16),
            vmem((BLOCK, BLOCK), BF16),
            vmem((HALVES, GROUPS, tok, WIDTH[0]), BF16),
            vmem((HALVES, GROUPS, tok, WIDTH[0]), BF16),
            vmem((HALVES, GROUPS // 2, tok, ROW), BF16),
            vmem((HALF_TOK, ROW), BF16),
            vmem((HALVES, HALF_TOK, ROW), BF16),
            vmem((HALVES, QUADS, 2, NX, 2, NZS, tok, BLOCK), BF16),
            vmem((HALVES, QUADS, 2, 2, 2, NZS, tok, BLOCK), BF16),
            vmem((HALVES, QUADS, 2, 2, NZS, tok, BLOCK), BF16),
            vmem((HALVES, QUADS, 2, 2, NZS, tok, BLOCK), BF16),
            vmem((HALVES, QUADS, NZS, 2, 2, tok, BLOCK), BF16),
            vmem((HALVES, QUADS, NZ - 1, 2, 2, tok, BLOCK), BF16),
            vmem((2, PAIRS * 16, BLOCK), BF16),
            dma((5,)),
            dma((SLOTS,)),
            dma((HALVES, GROUPS)),
            dma((HALVES, GROUPS)),
            dma((HALVES, GROUPS)),
            dma((HALVES, GROUPS)),
            dma((HALVES, QUADS, 2)),
            dma((HALVES, QUADS, 2)),
            dma((HALVES, QUADS, 2)),
            dma((HALVES, QUADS, 2)),
            dma((HALVES, QUADS, NZS)),
            dma((HALVES, QUADS, NZ - 1)),
        ],
        compiler_params=pltpu.CompilerParams(
            collective_id=0, has_side_effects=True, vmem_limit_bytes=60 * 1024 * 1024
        ),
        cost_estimate=pl.CostEstimate(flops=4_300_000_000, bytes_accessed=17_000_000, transcendentals=0),
    )(
        hidden.reshape(GROUPS, tok, ROW),
        residual,
        sign_bits,
        packed,
        scales,
        jnp.asarray(turn_table()),
    )


def solution(mesh):
    return jax.shard_map(
        shards,
        mesh=mesh,
        in_specs=(
            P("dp", "tensor"),
            P(("dp", "tensor"), None),
            P("tensor"),
            P("tensor", None),
            P(),
        ),
        out_specs=P(("dp", "tensor"), None),
        check_vma=False,
    )
```
